768 devices in a mesh: segment: 96 (over z_lo, y, x), head: 8 (over z_hi, core).
Axes of the slice: x: 4, y: 8, z: 12 (z_hi: 4, z_lo: 3; z = z_hi * 3 + z_lo), core: 2. Of those that a mesh axis runs over, the one named last changes fastest.
Arguments:
- grad_in: float32 [96, 128, 512], P('segment'), may hold values from -6 to 6
- memory: bfloat16 [96, 128, 512], P('segment'), may hold values from -120 to 120
- enc_grad_in: float32 [96, 128, 512], P('segment', None, 'head'), may hold values from -3 to 3
- act_stash: bfloat16 [96, 3, 128, 512], P('segment'), may hold values from -120 to 120
- slot_order: int32 [96, 3], P('segment'), may hold values from 0 to 2, each once within a row
- lengths: int32 [96, 3], P('segment'), may hold values from 16 to 128, as said below
- w_query: bfloat16 [96, 512, 8192], P('segment', None, 'head'), may hold values from -0.0234375 to 0.0234375
- w_key: bfloat16 [96, 512, 8192], P('segment', None, 'head'), may hold values from -0.25 to 0.25
- w_value: bfloat16 [96, 512, 8192], P('segment', None, 'head'), may hold values from -0.25 to 0.25
- w_out: bfloat16 [96, 8192, 512], P('segment', 'head'), may hold values from -0.0625 to 0.0625
Outputs:
- grad_out: float32 [96, 128, 512], P('segment')
- enc_grad_out: float32 [96, 128, 512], P('segment', None, 'head')
The draws below stay inside these ranges and needn't reach their ends.
Inputs may be any that keep to these rules, and one draw needn't show every extreme that they name: `slot_order`: each row lists every stash slot once. `lengths`: some entry equals 128.
All inputs are finite; a program needn't handle non-finite values.
Results may differ from the reference program's by a relative error of at most 0.018.
The reference program's roundings to bfloat16 on the way (of `decoded`, `queries`, `attention_low`, `context_grad`, `score_grad` and `query_grad`) count: a program that leaves them out, or rounds other values in their place, can miss the bound.
Values may be sent and summed in bfloat16 or wider, within the bound.
A program may use at most 32 MiB of HBM per device.

```python
import jax
import jax.numpy as jnp
from jax import lax

D = 512
HEAD_DIM = 128
DEC_ROWS = 128
ENC_ROWS = 128
TICKS = 3
HEADS = 64
SEGMENTS = 96


def scaled_rows(key, shape):
    base = jnp.clip(jax.random.normal(key, shape, jnp.float32), -5.0, 5.0)
    return base.astype(jnp.bfloat16)


def draw_memory(key, part):
    return scaled_rows(jax.random.fold_in(key, 11), (SEGMENTS, ENC_ROWS, D))


def draw_act_stash(key, part):
    return scaled_rows(jax.random.fold_in(key, 13), (SEGMENTS, TICKS, DEC_ROWS, D))


def draw_lengths(key, part):
    drawn = jax.random.randint(jax.random.fold_in(key, 17), (SEGMENTS, TICKS), ENC_ROWS // 8, ENC_ROWS + 1, jnp.int32)
    return drawn.at[0, 0].set(ENC_ROWS)


def shard_levels(key, dims, shards, smallest, high):
    gain = 1.0
    for position, blocks in shards:
        steps = jax.random.uniform(jax.random.fold_in(jax.random.fold_in(key, 6), position), (blocks,), jnp.float32, smallest / len(shards), high / len(shards))
        gain = gain * jnp.repeat(jnp.exp(steps), dims[position] // blocks).reshape((-1,) + (1,) * (len(dims) - 1 - position))
    return gain


def centred(stream_key, shape, spread, reach, pieces=(), kind=jnp.bfloat16):
    entries = spread * jax.random.normal(stream_key, shape, jnp.float32)
    if pieces:
        entries = entries * shard_levels(stream_key, shape, pieces, -0.22, 0.18)
    return jnp.clip(entries, -reach, reach).astype(kind)


def setup_inputs(seed: int = 0) -> dict:
    seeds = jax.random.split(jax.random.key(seed), 11)
    grad_in = centred(seeds[0], (SEGMENTS, DEC_ROWS, D), 1.0, 6.0, ((0, 96),), jnp.float32)
    memory = draw_memory(jax.random.fold_in(seeds[10], 71), 0)
    enc_grad_in = centred(seeds[2], (SEGMENTS, ENC_ROWS, D), 0.5, 3.0, ((0, 96), (2, 8)), jnp.float32)
    act_stash = draw_act_stash(jax.random.fold_in(seeds[10], 71), 0)
    slot_order = jax.vmap(lambda own: jax.random.permutation(own, TICKS))(jax.random.split(seeds[4], SEGMENTS)).reshape((SEGMENTS, TICKS)).astype(jnp.int32)
    lengths = draw_lengths(jax.random.fold_in(seeds[10], 71), 0)
    w_query = centred(seeds[6], (SEGMENTS, D, HEADS * HEAD_DIM), (D * HEAD_DIM) ** -0.5, 0.0234375, ((0, 96), (2, 8)))
    w_key = centred(seeds[7], (SEGMENTS, D, HEADS * HEAD_DIM), D ** -0.5, 0.25, ((0, 96), (2, 8)))
    w_value = centred(seeds[8], (SEGMENTS, D, HEADS * HEAD_DIM), D ** -0.5, 0.25, ((0, 96), (2, 8)))
    w_out = centred(seeds[9], (SEGMENTS, HEADS * HEAD_DIM, D), (HEADS * HEAD_DIM) ** -0.5, 0.0625, ((0, 96), (1, 8)))
    return {"grad_in": grad_in, "memory": memory, "enc_grad_in": enc_grad_in, "act_stash": act_stash, "slot_order": slot_order, "lengths": lengths, "w_query": w_query, "w_key": w_key, "w_value": w_value, "w_out": w_out}


def widened(values):
    return lax.optimization_barrier(values.astype(jnp.bfloat16)).astype(jnp.float32)


def segment_terms(gradient, held, decoded, length, w_query, w_key, w_value, w_out):
    inner = w_query.shape[1]
    head_total = inner // HEAD_DIM
    dec_rows = decoded.shape[0]
    enc_rows = held.shape[0]
    queries = jnp.dot(decoded, w_query, preferred_element_type=jnp.float32).astype(jnp.bfloat16)
    keys = jnp.dot(held, w_key, preferred_element_type=jnp.float32).astype(jnp.bfloat16)
    values = jnp.dot(held, w_value, preferred_element_type=jnp.float32).astype(jnp.bfloat16)
    query_heads = queries.astype(jnp.float32).reshape(dec_rows, head_total, HEAD_DIM)
    key_heads = keys.astype(jnp.float32).reshape(enc_rows, head_total, HEAD_DIM)
    value_heads = values.astype(jnp.float32).reshape(enc_rows, head_total, HEAD_DIM)
    scores = jnp.einsum("qhd,khd->hqk", query_heads, key_heads)
    allowed = jnp.arange(enc_rows, dtype=jnp.int32)[None, None, :] < length
    scores = jnp.where(allowed, scores, jnp.float32(-1e30))
    row_max = jnp.max(scores, axis=-1, keepdims=True)
    expo = jnp.exp(scores - row_max)
    attention = expo / jnp.sum(expo, axis=-1, keepdims=True)
    attention_low = widened(attention)
    context_grad = jnp.dot(gradient.astype(jnp.bfloat16), w_out.T, preferred_element_type=jnp.float32)
    context_heads = widened(context_grad).reshape(dec_rows, head_total, HEAD_DIM)
    prob_grad = jnp.einsum("qhd,khd->hqk", context_heads, value_heads)
    score_grad = widened(attention * (prob_grad - jnp.sum(attention * prob_grad, axis=-1, keepdims=True)))
    query_grad = widened(jnp.einsum("hqk,khd->qhd", score_grad, key_heads)).reshape(dec_rows, inner)
    key_grad = widened(jnp.einsum("hqk,qhd->khd", score_grad, query_heads)).reshape(enc_rows, inner)
    value_grad = widened(jnp.einsum("hqk,qhd->khd", attention_low, context_heads)).reshape(enc_rows, inner)
    decoder_grad = jnp.dot(query_grad, w_query.astype(jnp.float32).T)
    memory_grad = jnp.dot(key_grad, w_key.astype(jnp.float32).T) + jnp.dot(value_grad, w_value.astype(jnp.float32).T)
    return decoder_grad, memory_grad


def reference(grad_in, memory, enc_grad_in, act_stash, slot_order, lengths, w_query, w_key, w_value, w_out):
    gradient = grad_in
    carried = enc_grad_in
    held = memory
    section_ids = jnp.arange(grad_in.shape[0], dtype=jnp.int32)
    for tick_index in range(TICKS):
        decoded = act_stash[section_ids, slot_order[:, tick_index].astype(jnp.int32)]

        def per_segment(operands):
            return segment_terms(*operands)

        decoder_grad, memory_grad = lax.map(per_segment, (gradient, held, decoded, lengths[:, tick_index], w_query, w_key, w_value, w_out))
        gradient = jnp.roll(gradient + decoder_grad, -1, axis=0)
        carried = jnp.roll(carried + memory_grad, -1, axis=0)
        if tick_index + 1 < TICKS:
            held = jnp.roll(held, -1, axis=0)
    return gradient, carried
```

```python
import jax
import jax.numpy as jnp
from jax import lax
from jax.experimental import pallas as pl
from jax.experimental.pallas import tpu as pltpu
from jax.sharding import PartitionSpec as P

HEAD_DIM = 128
TICKS = 3
MESH = pl.DeviceIdType.MESH
F32 = jnp.float32
BF16 = jnp.bfloat16
ORDER = (0, 2, 1, 3)


def nn(a, b):
    return lax.dot_general(a, b, (((1,), (0,)), ((), ())), preferred_element_type=F32)


def nt(a, b):
    return lax.dot_general(a, b, (((1,), (1,)), ((), ())), preferred_element_type=F32)


def tn(a, b):
    return lax.dot_general(a, b, (((0,), (0,)), ((), ())), preferred_element_type=F32)


def kernel(
    grad_hbm, mem_hbm, enc_hbm, stash_hbm, slot_ref, len_ref, wq_hbm, wk_hbm, wv_hbm, wo_hbm,
    gout_ref, eout_ref,
    grad_v, stash_v, wq, wk, wv, wo, held, q_s, k_s, v_s, att, cg_s, sg_s, qg_s, kg_s, vg_s,
    gl, gres, dpf, dpb, sibr, r1s, r1r, r2s, r2x, r2y, gfin,
    mpf, mpb, mpr, cs, cr, fin, esw, esr, encr,
    load_sem, sib_s, sib_r, r1_ss, r1_rs, x_ss, x_rs, y_ss, y_rs, fw_ss, fw_rs,
    mp_ss, mp_rs, c_ss, c_rs, f_ss, f_rs, h_ss, h_rs, hf_ss, hf_rs, e_ss, e_rs, w_ss, w_rs,
):
    heads = wq.shape[1] // HEAD_DIM
    seg = lax.axis_index("segment")
    head = lax.axis_index("head")
    segments = lax.axis_size("segment")
    c = head // 2
    k = head % 2
    prev = (seg + segments - 1) % segments
    prev3 = (seg + 3 * segments - 3) % segments
    nxt = (seg + 1) % segments
    nxt3 = (seg + 3) % segments
    c1 = c + 1 - 2 * (c % 2)
    c3 = 3 - c
    sib = (seg, 2 * c + 1 - k)
    mine = pl.ds(pl.multiple_of(64 * k, 64), 64)
    other = pl.ds(pl.multiple_of(64 * (1 - k), 64), 64)

    def rcopy(src, dst, ss, rs, dev):
        return pltpu.make_async_remote_copy(
            src_ref=src, dst_ref=dst, send_sem=ss, recv_sem=rs, device_id=dev, device_id_type=MESH
        )

    sends = []

    def go(copy):
        copy.start()
        sends.append(copy)
        return copy

    loads = {}

    def load(name, src, dst):
        copy = pltpu.make_async_copy(src, dst, load_sem.at[len(loads)])
        copy.start()
        loads[name] = copy

    load("mem", mem_hbm.at[0], held.at[0])
    load("wk", wk_hbm.at[0], wk)
    load("stash", stash_hbm.at[0], stash_v)
    load("wq", wq_hbm.at[0], wq)
    load("wv", wv_hbm.at[0], wv)
    load("grad", grad_hbm.at[0], grad_v)
    load("wo", wo_hbm.at[0], wo)

    barrier = pltpu.get_barrier_semaphore()
    senders = [sib, (seg, 2 * c1 + k), (seg, 2 * c3 + k), (nxt3, head)]
    senders += [(nxt, 2 * ((c + r) % 4) + k) for r in range(4)]
    for dev in senders:
        pl.semaphore_signal(barrier, inc=1, device_id=dev, device_id_type=MESH)

    def keys_of(t):
        k_s[...] = jnp.concatenate(
            [nn(held[t], wk[:, 256 * n : 256 * n + 256]).astype(BF16) for n in range(4)], axis=1
        )

    def values_of(t):
        v_s[...] = jnp.concatenate(
            [nn(held[t], wv[:, 256 * n : 256 * n + 256]).astype(BF16) for n in range(4)], axis=1
        )

    def queries_of(t):
        decoded = stash_v[slot_ref[0, t]]
        q_s[...] = jnp.concatenate(
            [nn(decoded, wq[:, 256 * n : 256 * n + 256]).astype(BF16) for n in range(4)], axis=1
        )

    def softmax_of(t):
        allowed = lax.broadcasted_iota(jnp.int32, (128, 128), 1) < len_ref[0, t]
        for h in range(heads):
            at = slice(HEAD_DIM * h, HEAD_DIM * h + HEAD_DIM)
            scores = jnp.where(allowed, nt(q_s[:, at], k_s[:, at]), F32(-1e30))
            expo = jnp.exp(scores - jnp.max(scores, axis=-1, keepdims=True))
            att[h] = expo / jnp.sum(expo, axis=-1, keepdims=True)

    loads["mem"].wait()
    loads["wk"].wait()
    keys_of(0)
    loads["stash"].wait()
    loads["wq"].wait()
    queries_of(0)

    pl.semaphore_wait(barrier, 8)
    helds = [
        rcopy(held.at[t, mine], held.at[t + 1, mine], h_ss.at[t], h_rs.at[t], (prev, head))
        for t in range(TICKS - 1)
    ]
    held_fw = [
        rcopy(held.at[t + 1, mine], held.at[t + 1, mine], hf_ss.at[t], hf_rs.at[t], sib)
        for t in range(TICKS - 1)
    ]
    go(helds[0])
    enc_copy = go(rcopy(enc_hbm.at[0], encr, e_ss, e_rs, (prev3, head)))

    softmax_of(0)
    loads["wv"].wait()
    values_of(0)
    loads["grad"].wait()
    for j in range(4):
        cols = slice(128 * j, 128 * j + 128)
        gl[0, j] = grad_v[:, cols].astype(BF16)
        gres[j] = grad_v[mine, cols]
    loads["wo"].wait()

    for t in range(TICKS):
        last = t == TICKS - 1
        g = jnp.concatenate([gl[t, j] for j in range(4)], axis=1)
        for n in range(4):
            cg_s[:, 256 * n : 256 * n + 256] = nt(g, wo[256 * n : 256 * n + 256, :]).astype(BF16)
        for h in range(heads):
            at = slice(HEAD_DIM * h, HEAD_DIM * h + HEAD_DIM)
            prob_grad = nt(cg_s[:, at], v_s[:, at])
            weight = att[h]
            total = jnp.sum(weight * prob_grad, axis=-1, keepdims=True)
            score_grad = (weight * (prob_grad - total)).astype(BF16)
            sg_s[h] = score_grad
            qg_s[:, at] = nn(score_grad, k_s[:, at]).astype(BF16)
        pair = {}
        for j in ORDER:
            part = nt(qg_s[...], wq[128 * j : 128 * j + 128, :])
            dpf[j] = part
            dpb[t, j] = part.astype(BF16)
            pair[j] = go(
                rcopy(dpb.at[t, j, other], sibr.at[t, j], sib_s.at[t, j], sib_r.at[t, j], sib)
            )
        first = {}
        for j in ORDER:
            pair[j].wait_recv()
            r1s[t, j] = (dpf[j, mine] + sibr[t, j].astype(F32)).astype(BF16)
            partner = c1 if j < 2 else c3
            first[j] = go(
                rcopy(
                    r1s.at[t, j], r1r.at[t, j], r1_ss.at[t, j], r1_rs.at[t, j],
                    (seg, 2 * partner + k),
                )
            )
        for h in range(heads):
            at = slice(HEAD_DIM * h, HEAD_DIM * h + HEAD_DIM)
            vg_s[:, at] = tn(att[h].astype(BF16), cg_s[:, at]).astype(BF16)
            kg_s[:, at] = tn(sg_s[h], q_s[:, at]).astype(BF16)
        for j in range(4):
            rows = slice(128 * j, 128 * j + 128)
            part = nt(kg_s[...], wk[rows, :]) + nt(vg_s[...], wv[rows, :])
            mpf[j] = part
            mpb[t, j] = part.astype(BF16)
        mp_copy = go(rcopy(mpb.at[t, :, other], mpr.at[t], mp_ss.at[t], mp_rs.at[t], sib))

        def carry():
            mp_copy.wait_recv()
            if t > 0:
                carried[t - 1].wait_recv()
            for j in range(4):
                part = mpf[j, mine] + mpr[t, j].astype(F32)
                if t > 0:
                    part = part + cr[t - 1, j].astype(F32)
                cs[t, j] = part.astype(BF16)

        if t == 0:
            carried = [
                rcopy(cs.at[i], cr.at[i], c_ss.at[i], c_rs.at[i], (prev, head))
                for i in range(TICKS - 1)
            ]
        if not last:
            helds[t].wait_recv()
            go(held_fw[t])
            if t + 1 < TICKS - 1:
                go(helds[t + 1])
            held_fw[t].wait_recv()
            keys_of(t + 1)
            values_of(t + 1)
        else:
            carry()
            final = []
            for r in range(4):
                dest = (c + r) % 4
                final.append(
                    go(rcopy(cs.at[t, dest], fin.at[r], f_ss.at[r], f_rs.at[r], (prev, 2 * dest + k)))
                )
        straight, across = {}, {}
        for j in ORDER:
            first[j].wait_recv()
            side = (c // 2) if j < 2 else ((c + 1) // 2) % 2
            keep = jnp.where(side == 0, F32(1.0), F32(0.0))
            total = r1s[t, j].astype(F32) + r1r[t, j].astype(F32) + keep * gres[j]
            r2s[t, j] = total.astype(BF16)
            partner = c3 if j < 2 else c1
            across[j] = go(
                rcopy(
                    r2s.at[t, j], r2y.at[t, j], y_ss.at[t, j], y_rs.at[t, j],
                    (prev, 2 * partner + k),
                )
            )
            straight[j] = go(
                rcopy(r2s.at[t, j], r2x.at[t, j], x_ss.at[t, j], x_rs.at[t, j], (prev, head))
            )
        if not last:
            carry()
            go(carried[t])
            queries_of(t + 1)
            softmax_of(t + 1)
        else:
            for r in range(4):
                final[r].wait_recv()
            total = fin[0].astype(F32) + fin[1].astype(F32) + fin[2].astype(F32) + fin[3].astype(F32)
            esw[...] = total
            swap = go(rcopy(esw, esr, w_ss, w_rs, sib))
        forward = {}
        for j in ORDER:
            straight[j].wait_recv()
            across[j].wait_recv()
            total = r2x[t, j].astype(F32) + r2y[t, j].astype(F32)
            if last:
                gfin[j, mine] = total
                part = gfin.at[j, mine]
            else:
                gres[j] = total
                gl[t + 1, j, mine] = total.astype(BF16)
                part = gl.at[t + 1, j, mine]
            forward[j] = go(rcopy(part, part, fw_ss.at[t, j], fw_rs.at[t, j], sib))
        for j in ORDER:
            forward[j].wait_recv()

    for j in range(4):
        gout_ref[0, :, 128 * j : 128 * j + 128] = gfin[j]
    swap.wait_recv()
    enc_copy.wait_recv()

    def my_columns(x):
        return jnp.where(k == 0, x[:, :64], x[:, 64:])

    eout_ref[0, mine, :] = encr[mine, :] + my_columns(esw[...])
    eout_ref[0, other, :] = encr[other, :] + my_columns(esr[...])
    for copy in sends:
        copy.wait_send()


def body(
    grad_in, memory, enc_grad_in, act_stash, slot_order, lengths, w_query, w_key, w_value, w_out
):
    inner = w_query.shape[2]
    heads = inner // HEAD_DIM
    anywhere = pl.BlockSpec(memory_space=pl.ANY)
    scalars = pl.BlockSpec(memory_space=pltpu.SMEM)
    whole = pl.BlockSpec(memory_space=pltpu.VMEM)

    def dma(*shape):
        return pltpu.SemaphoreType.DMA(shape) if shape else pltpu.SemaphoreType.DMA

    V = pltpu.VMEM
    half = (64, 128)
    scratch = [
        V((128, 512), F32), V((TICKS, 128, 512), BF16),
        V((512, inner), BF16), V((512, inner), BF16), V((512, inner), BF16), V((inner, 512), BF16),
        V((TICKS, 128, 512), BF16),
        V((128, inner), BF16), V((128, inner), BF16), V((128, inner), BF16),
        V((heads, 128, 128), F32),
        V((128, inner), BF16), V((heads, 128, 128), BF16),
        V((128, inner), BF16), V((128, inner), BF16), V((128, inner), BF16),
        V((TICKS, 4, 128, 128), BF16), V((4, *half), F32),
        V((4, 128, 128), F32), V((TICKS, 4, 128, 128), BF16), V((TICKS, 4, *half), BF16),
        V((TICKS, 4, *half), BF16), V((TICKS, 4, *half), BF16),
        V((TICKS, 4, *half), BF16), V((TICKS, 4, *half), BF16), V((TICKS, 4, *half), BF16),
        V((4, 128, 128), F32),
        V((4, 128, 128), F32), V((TICKS, 4, 128, 128), BF16), V((TICKS, 4, *half), BF16),
        V((TICKS, 4, *half), BF16), V((TICKS - 1, 4, *half), BF16),
        V((4, *half), BF16), V(half, F32), V(half, F32), V((128, 64), F32),
        dma(7),
        dma(TICKS, 4), dma(TICKS, 4), dma(TICKS, 4), dma(TICKS, 4),
        dma(TICKS, 4), dma(TICKS, 4), dma(TICKS, 4), dma(TICKS, 4), dma(TICKS, 4), dma(TICKS, 4),
        dma(TICKS), dma(TICKS), dma(TICKS - 1), dma(TICKS - 1), dma(4), dma(4),
        dma(TICKS - 1), dma(TICKS - 1), dma(TICKS - 1), dma(TICKS - 1), dma(), dma(), dma(), dma(),
    ]
    return pl.pallas_call(
        kernel,
        name="relay_backward",
        out_shape=(
            jax.ShapeDtypeStruct(grad_in.shape, F32),
            jax.ShapeDtypeStruct(enc_grad_in.shape, F32),
        ),
        in_specs=[anywhere] * 4 + [scalars] * 2 + [anywhere] * 4,
        out_specs=(whole, whole),
        scratch_shapes=scratch,
        compiler_params=pltpu.CompilerParams(
            collective_id=0, has_side_effects=True, vmem_limit_bytes=40 * 1024 * 1024
        ),
        cost_estimate=pl.CostEstimate(
            flops=3_400_000_000, bytes_accessed=5_500_000, transcendentals=400_000
        ),
    )(grad_in, memory, enc_grad_in, act_stash, slot_order, lengths, w_query, w_key, w_value, w_out)


def solution(mesh):
    in_specs = (
        P("segment", None, None),
        P("segment", None, None),
        P("segment", None, "head"),
        P("segment", None, None, None),
        P("segment", None),
        P("segment", None),
        P("segment", None, "head"),
        P("segment", None, "head"),
        P("segment", None, "head"),
        P("segment", "head", None),
    )
    out_specs = (P("segment", None, None), P("segment", None, "head"))
    return jax.shard_map(body, mesh=mesh, in_specs=in_specs, out_specs=out_specs, check_vma=False)
```

```python
import jax
import jax.numpy as jnp
from jax import lax
from jax.experimental import pallas as pl
from jax.experimental.pallas import tpu as pltpu
from jax.sharding import PartitionSpec as P

HEAD_DIM = 128
TICKS = 3
MESH = pl.DeviceIdType.MESH
F32 = jnp.float32
BF16 = jnp.bfloat16
ORDER = (0, 1, 2, 3)


def nn(a, b):
    return lax.dot_general(a, b, (((1,), (0,)), ((), ())), preferred_element_type=F32)


def nt(a, b):
    return lax.dot_general(a, b, (((1,), (1,)), ((), ())), preferred_element_type=F32)


def tn(a, b):
    return lax.dot_general(a, b, (((0,), (0,)), ((), ())), preferred_element_type=F32)


def kernel(
    grad_hbm, mem_hbm, enc_hbm, stash_hbm, slot_ref, len_ref, wq_hbm, wk_hbm, wv_hbm, wo_hbm,
    gout_ref, eout_ref,
    grad_v, stash_v, wq, wk, wv, wo, held, q_s, k_s, v_s, wot, wqt, att, cg_s, sg_s, kg_s, vg_s,
    gl, gres, dpf, dpb, sibr, r1s, r1r, r2s, r2x, r2y, gfin,
    mpf, mpb, mpr, cs, cr, fin, encr,
    load_sem, sib_s, sib_r, r1_ss, r1_rs, x_ss, x_rs, y_ss, y_rs, fw_ss, fw_rs,
    mp_ss, mp_rs, c_ss, c_rs, f_ss, f_rs, h_ss, h_rs, hf_ss, hf_rs, e_ss, e_rs,
):
    heads = wq.shape[1] // HEAD_DIM
    seg = lax.axis_index("segment")
    head = lax.axis_index("head")
    segments = lax.axis_size("segment")
    c = head // 2
    k = head % 2
    prev = (seg + segments - 1) % segments
    prev3 = (seg + 3 * segments - 3) % segments
    nxt = (seg + 1) % segments
    nxt3 = (seg + 3) % segments
    c1 = c + 1 - 2 * (c % 2)
    c3 = 3 - c
    sib = (seg, 2 * c + 1 - k)
    mine = pl.ds(pl.multiple_of(64 * k, 64), 64)
    other = pl.ds(pl.multiple_of(64 * (1 - k), 64), 64)

    def rcopy(src, dst, ss, rs, dev):
        return pltpu.make_async_remote_copy(
            src_ref=src, dst_ref=dst, send_sem=ss, recv_sem=rs, device_id=dev, device_id_type=MESH
        )

    sends = []

    def go(copy):
        copy.start()
        sends.append(copy)
        return copy

    loads = {}

    def load(name, src, dst):
        copy = pltpu.make_async_copy(src, dst, load_sem.at[len(loads)])
        copy.start()
        loads[name] = copy

    load("mem", mem_hbm.at[0], held.at[0])
    load("wk", wk_hbm.at[0], wk)
    load("stash", stash_hbm.at[0], stash_v)
    load("wq", wq_hbm.at[0], wq)
    load("wv", wv_hbm.at[0], wv)
    load("grad", grad_hbm.at[0], grad_v)
    load("wo", wo_hbm.at[0], wo)

    barrier = pltpu.get_barrier_semaphore()
    senders = [sib, (seg, 2 * c1 + k), (seg, 2 * c3 + k), (nxt3, head)]
    senders += [(nxt, 2 * ((c + r) % 4) + k) for r in range(4)]
    for dev in senders:
        pl.semaphore_signal(barrier, inc=1, device_id=dev, device_id_type=MESH)

    def at(h):
        return slice(HEAD_DIM * h, HEAD_DIM * h + HEAD_DIM)

    def keys_of(t):
        k_s[...] = jnp.concatenate(
            [nn(held[t], wk[:, 256 * n : 256 * n + 256]).astype(BF16) for n in range(4)], axis=1
        )

    def values_of(t):
        v_s[...] = jnp.concatenate(
            [nn(held[t], wv[:, 256 * n : 256 * n + 256]).astype(BF16) for n in range(4)], axis=1
        )

    def queries_of(t):
        decoded = stash_v[slot_ref[0, t]]
        q_s[...] = jnp.concatenate(
            [nn(decoded, wq[:, 256 * n : 256 * n + 256]).astype(BF16) for n in range(4)], axis=1
        )

    def softmax_of(t):
        allowed = lax.broadcasted_iota(jnp.int32, (128, 128), 1) < len_ref[0, t]
        scores = [nt(q_s[:, at(h)], k_s[:, at(h)]) for h in range(heads)]
        weights = []
        for h in range(heads):
            score = jnp.where(allowed, scores[h], F32(-1e30))
            expo = jnp.exp(score - jnp.max(score, axis=-1, keepdims=True))
            weights.append(expo / jnp.sum(expo, axis=-1, keepdims=True))
        for h in range(heads):
            att[h] = weights[h]

    loads["mem"].wait()
    loads["wk"].wait()
    keys_of(0)
    loads["stash"].wait()
    loads["wq"].wait()
    queries_of(0)

    pl.semaphore_wait(barrier, 8)
    helds = [
        rcopy(held.at[t, mine], held.at[t + 1, mine], h_ss.at[t], h_rs.at[t], (prev, head))
        for t in range(TICKS - 1)
    ]
    held_fw = [
        rcopy(held.at[t + 1, mine], held.at[t + 1, mine], hf_ss.at[t], hf_rs.at[t], sib)
        for t in range(TICKS - 1)
    ]
    go(helds[0])
    enc_copy = go(rcopy(enc_hbm.at[0], encr, e_ss, e_rs, (prev3, head)))

    softmax_of(0)
    loads["wv"].wait()
    values_of(0)
    loads["grad"].wait()
    for j in range(4):
        cols = slice(128 * j, 128 * j + 128)
        gl[0, j] = grad_v[:, cols].astype(BF16)
        gres[j] = grad_v[mine, cols]
    loads["wo"].wait()

    for t in range(TICKS):
        last = t == TICKS - 1
        g = jnp.concatenate([gl[t, j] for j in range(4)], axis=1)
        if t == 0:
            context = [nt(g, wo[256 * n : 256 * n + 256, :]).astype(BF16) for n in range(4)]
        else:
            context = [nn(g, wot[:, 256 * n : 256 * n + 256]).astype(BF16) for n in range(4)]
        cg_s[...] = jnp.concatenate(context, axis=1)
        prob_grads = [nt(cg_s[:, at(h)], v_s[:, at(h)]) for h in range(heads)]
        score_grads = []
        for h in range(heads):
            weight = att[h]
            total = jnp.sum(weight * prob_grads[h], axis=-1, keepdims=True)
            score_grads.append((weight * (prob_grads[h] - total)).astype(BF16))
        query_grads = [nn(score_grads[h], k_s[:, at(h)]).astype(BF16) for h in range(heads)]
        for h in range(heads):
            sg_s[h] = score_grads[h]
        query_grad = jnp.concatenate(query_grads, axis=1)
        pair = {}
        for n in range(2):
            cols = slice(256 * n, 256 * n + 256)
            if t == 0:
                part = nt(query_grad, wq[cols, :])
            else:
                part = nn(query_grad, wqt[:, cols])
            for j in (2 * n, 2 * n + 1):
                piece = part[:, 128 * (j - 2 * n) : 128 * (j - 2 * n) + 128]
                dpf[j] = piece
                dpb[t, j] = piece.astype(BF16)
                pair[j] = go(
                    rcopy(dpb.at[t, j, other], sibr.at[t, j], sib_s.at[t, j], sib_r.at[t, j], sib)
                )
        first = {}
        for j in ORDER:
            pair[j].wait_recv()
            r1s[t, j] = (dpf[j, mine] + sibr[t, j].astype(F32)).astype(BF16)
            partner = c1 if j < 2 else c3
            first[j] = go(
                rcopy(
                    r1s.at[t, j], r1r.at[t, j], r1_ss.at[t, j], r1_rs.at[t, j],
                    (seg, 2 * partner + k),
                )
            )
        value_grads = [tn(att[h].astype(BF16), cg_s[:, at(h)]).astype(BF16) for h in range(heads)]
        key_grads = [tn(sg_s[h], q_s[:, at(h)]).astype(BF16) for h in range(heads)]
        vg_s[...] = jnp.concatenate(value_grads, axis=1)
        kg_s[...] = jnp.concatenate(key_grads, axis=1)
        for j in range(4):
            rows = slice(128 * j, 128 * j + 128)
            part = nt(wk[rows, :], kg_s[...]) + nt(wv[rows, :], vg_s[...])
            mpf[j] = part
            mpb[t, j] = part.astype(BF16)
        mp_copy = go(rcopy(mpb.at[t, :, other], mpr.at[t], mp_ss.at[t], mp_rs.at[t], sib))

        def carry():
            mp_copy.wait_recv()
            if t > 0:
                carried[t - 1].wait_recv()
            for j in range(4):
                part = mpf[j, mine] + mpr[t, j].astype(F32)
                if t > 0:
                    part = part + cr[t - 1, j].astype(F32)
                cs[t, j] = part.astype(BF16)

        if t == 0:
            carried = [
                rcopy(cs.at[i], cr.at[i], c_ss.at[i], c_rs.at[i], (prev, head))
                for i in range(TICKS - 1)
            ]
        if t == 0:
            for n in range(8):
                cols = slice(128 * n, 128 * n + 128)
                wot[:, cols] = wo[cols, :].T
                wqt[cols, :] = wq[:, cols].T
        if not last:
            helds[t].wait_recv()
            go(held_fw[t])
            if t + 1 < TICKS - 1:
                go(helds[t + 1])
            held_fw[t].wait_recv()
            keys_of(t + 1)
            values_of(t + 1)
        else:
            carry()
            final = []
            for r in range(4):
                dest = (c + r) % 4
                final.append(
                    go(rcopy(cs.at[t, dest], fin.at[r], f_ss.at[r], f_rs.at[r], (prev, 2 * dest + k)))
                )
        straight, across = {}, {}
        for j in ORDER:
            first[j].wait_recv()
            side = (c // 2) if j < 2 else ((c + 1) // 2) % 2
            keep = jnp.where(side == 0, F32(1.0), F32(0.0))
            total = r1s[t, j].astype(F32) + r1r[t, j].astype(F32) + keep * gres[j]
            r2s[t, j] = total.astype(BF16)
            partner = c3 if j < 2 else c1
            across[j] = go(
                rcopy(
                    r2s.at[t, j], r2y.at[t, j], y_ss.at[t, j], y_rs.at[t, j],
                    (prev, 2 * partner + k),
                )
            )
            straight[j] = go(
                rcopy(r2s.at[t, j], r2x.at[t, j], x_ss.at[t, j], x_rs.at[t, j], (prev, head))
            )
        if not last:
            carry()
            go(carried[t])
            queries_of(t + 1)
            softmax_of(t + 1)
        else:
            for r in range(4):
                final[r].wait_recv()
            enc_copy.wait_recv()
            total = fin[0].astype(F32) + fin[1].astype(F32) + fin[2].astype(F32) + fin[3].astype(F32)
            eout_ref[0] = encr[...] + total
        forward = {}
        for j in ORDER:
            straight[j].wait_recv()
            across[j].wait_recv()
            total = r2x[t, j].astype(F32) + r2y[t, j].astype(F32)
            if last:
                gfin[j, mine] = total
                part = gfin.at[j, mine]
            else:
                gres[j] = total
                gl[t + 1, j, mine] = total.astype(BF16)
                part = gl.at[t + 1, j, mine]
            forward[j] = go(rcopy(part, part, fw_ss.at[t, j], fw_rs.at[t, j], sib))
        for j in ORDER:
            forward[j].wait_recv()

    for j in range(4):
        gout_ref[0, :, 128 * j : 128 * j + 128] = gfin[j]
    for copy in sends:
        copy.wait_send()


def body(
    grad_in, memory, enc_grad_in, act_stash, slot_order, lengths, w_query, w_key, w_value, w_out
):
    inner = w_query.shape[2]
    heads = inner // HEAD_DIM
    anywhere = pl.BlockSpec(memory_space=pl.ANY)
    scalars = pl.BlockSpec(memory_space=pltpu.SMEM)
    whole = pl.BlockSpec(memory_space=pltpu.VMEM)

    def dma(*shape):
        return pltpu.SemaphoreType.DMA(shape) if shape else pltpu.SemaphoreType.DMA

    V = pltpu.VMEM
    half = (64, 128)
    scratch = [
        V((128, 512), F32), V((TICKS, 128, 512), BF16),
        V((512, inner), BF16), V((512, inner), BF16), V((512, inner), BF16), V((inner, 512), BF16),
        V((TICKS, 128, 512), BF16),
        V((128, inner), BF16), V((128, inner), BF16), V((128, inner), BF16),
        V((512, inner), BF16), V((inner, 512), BF16),
        V((heads, 128, 128), F32),
        V((128, inner), BF16), V((heads, 128, 128), BF16),
        V((128, inner), BF16), V((128, inner), BF16),
        V((TICKS, 4, 128, 128), BF16), V((4, *half), F32),
        V((4, 128, 128), F32), V((TICKS, 4, 128, 128), BF16), V((TICKS, 4, *half), BF16),
        V((TICKS, 4, *half), BF16), V((TICKS, 4, *half), BF16),
        V((TICKS, 4, *half), BF16), V((TICKS, 4, *half), BF16), V((TICKS, 4, *half), BF16),
        V((4, 128, 128), F32),
        V((4, 128, 128), F32), V((TICKS, 4, 128, 128), BF16), V((TICKS, 4, *half), BF16),
        V((TICKS, 4, *half), BF16), V((TICKS - 1, 4, *half), BF16),
        V((4, *half), BF16), V(half, F32),
        dma(7),
        dma(TICKS, 4), dma(TICKS, 4), dma(TICKS, 4), dma(TICKS, 4),
        dma(TICKS, 4), dma(TICKS, 4), dma(TICKS, 4), dma(TICKS, 4), dma(TICKS, 4), dma(TICKS, 4),
        dma(TICKS), dma(TICKS), dma(TICKS - 1), dma(TICKS - 1), dma(4), dma(4),
        dma(TICKS - 1), dma(TICKS - 1), dma(TICKS - 1), dma(TICKS - 1), dma(), dma(),
    ]
    enc_turned = jnp.swapaxes(enc_grad_in, 1, 2)
    grad_out, enc_out = pl.pallas_call(
        kernel,
        name="relay_backward",
        out_shape=(
            jax.ShapeDtypeStruct(grad_in.shape, F32),
            jax.ShapeDtypeStruct(enc_turned.shape, F32),
        ),
        in_specs=[anywhere] * 4 + [scalars] * 2 + [anywhere] * 4,
        out_specs=(whole, whole),
        scratch_shapes=scratch,
        compiler_params=pltpu.CompilerParams(
            collective_id=0, has_side_effects=True, vmem_limit_bytes=56 * 1024 * 1024
        ),
        cost_estimate=pl.CostEstimate(
            flops=3_400_000_000, bytes_accessed=5_500_000, transcendentals=400_000
        ),
    )(grad_in, memory, enc_turned, act_stash, slot_order, lengths, w_query, w_key, w_value, w_out)
    return grad_out, jnp.swapaxes(enc_out, 1, 2)


def solution(mesh):
    in_specs = (
        P("segment", None, None),
        P("segment", None, None),
        P("segment", None, "head"),
        P("segment", None, None, None),
        P("segment", None),
        P("segment", None),
        P("segment", None, "head"),
        P("segment", None, "head"),
        P("segment", None, "head"),
        P("segment", "head", None),
    )
    out_specs = (P("segment", None, None), P("segment", None, "head"))
    return jax.shard_map(body, mesh=mesh, in_specs=in_specs, out_specs=out_specs, check_vma=False)
```

```python
import types

import jax
import jax.numpy as jnp
from jax import lax
from jax.experimental import pallas as pl
from jax.experimental.pallas import tpu as pltpu
from jax.sharding import PartitionSpec as P

HEAD_DIM = 128
TICKS = 3
MESH = pl.DeviceIdType.MESH
F32 = jnp.float32
BF16 = jnp.bfloat16
EARLY = ()
FIRST_ORDER = (0, 1, 2, 3)
SECOND_ORDER = (0, 1, 2, 3)


def nn(a, b):
    return lax.dot_general(a, b, (((1,), (0,)), ((), ())), preferred_element_type=F32)


def nt(a, b):
    return lax.dot_general(a, b, (((1,), (1,)), ((), ())), preferred_element_type=F32)


def tn(a, b):
    return lax.dot_general(a, b, (((0,), (0,)), ((), ())), preferred_element_type=F32)


def at(h):
    return slice(HEAD_DIM * h, HEAD_DIM * h + HEAD_DIM)


def wide(a, w):
    return [nn(a, w[:, 256 * n : 256 * n + 256]).astype(BF16) for n in range(w.shape[1] // 256)]


def joined(pieces):
    return jnp.concatenate(pieces, axis=1)


def scratch_spec(inner):
    heads = inner // HEAD_DIM
    half = (64, 128)

    def v(shape, kind):
        return pltpu.VMEM(shape, kind)

    def s(*shape):
        return pltpu.SemaphoreType.DMA(shape) if shape else pltpu.SemaphoreType.DMA

    spec = dict(
        grad=v((128, 512), F32), stash=v((TICKS, 128, 512), BF16),
        wq=v((512, inner), BF16), wk=v((512, inner), BF16), wv=v((512, inner), BF16),
        wo=v((inner, 512), BF16), wot=v((2, 512, inner), BF16), wqt=v((2, inner, 512), BF16),
        wk2=v((512, inner), BF16), wv2=v((512, inner), BF16),
        held=v((TICKS, 128, 512), BF16),
        q=v((TICKS, 128, inner), BF16), k=v((TICKS, 2, 128, inner), BF16),
        v=v((TICKS, 2, 128, inner), BF16), q2=v((TICKS, 64, inner), BF16),
        att=v((heads, 128, 128), F32), att2=v((2 * heads, 64, 128), F32),
        cg=v((128, inner), BF16), sg=v((heads, 128, 128), BF16),
        cg2=v((2, 64, inner), BF16), cgf=v((2, 64, inner), F32), sg2=v((2 * heads, 64, 128), BF16),
        kg=v((2, 128, inner), BF16), vg=v((2, 128, inner), BF16),
        gres=v((8, 32, 128), F32), dpf=v((4, 128, 128), F32), dpb=v((4, 128, 128), BF16),
        sibr=v((4, *half), BF16),
        r1s=v((TICKS, 8, 32, 128), BF16), r1r=v((TICKS, 8, 32, 128), BF16),
        r2s=v((TICKS, 8, 32, 128), BF16), r2x=v((TICKS, 8, 32, 128), BF16),
        r2y=v((TICKS, 8, 32, 128), BF16), gfin=v((4, *half), F32),
        mpf=v((4, 128, 128), F32), mpb=v((TICKS, 4, 128, 128), BF16),
        mpr=v((TICKS, 4, *half), BF16), cs=v((TICKS, 4, *half), BF16),
        cr=v((TICKS - 1, 4, *half), BF16), fin=v((4, *half), BF16), encr=v(half, F32),
        load=s(7),
    )
    for name, shape in dict(
        sib=(4,), r1=(TICKS, 8), x=(TICKS, 8), y=(TICKS, 8), fw=(4,), mp=(TICKS,), c=(TICKS - 1,),
        f=(4,), h=(TICKS - 1,), hf=(TICKS - 1,), e=(), w=(4,), kk=(TICKS,), vv=(TICKS,), qq=(TICKS,),
    ).items():
        spec[name + "_ss"] = s(*shape)
        spec[name + "_rs"] = s(*shape)
    return spec


def kernel(
    names, grad_hbm, mem_hbm, enc_hbm, stash_hbm, slot_ref, len_ref, wq_hbm, wk_hbm, wv_hbm, wo_hbm,
    gout_ref, eout_ref, *scratch
):
    z = types.SimpleNamespace(**dict(zip(names, scratch)))
    heads = z.wq.shape[1] // HEAD_DIM
    seg = lax.axis_index("segment")
    head = lax.axis_index("head")
    segments = lax.axis_size("segment")
    c = head // 2
    k = head % 2
    prev = (seg + segments - 1) % segments
    prev3 = (seg + 3 * segments - 3) % segments
    nxt = (seg + 1) % segments
    nxt3 = (seg + 3) % segments
    c1 = c + 1 - 2 * (c % 2)
    c3 = 3 - c
    sib = (seg, 2 * c + 1 - k)
    mine = pl.ds(pl.multiple_of(64 * k, 64), 64)
    other = pl.ds(pl.multiple_of(64 * (1 - k), 64), 64)

    def rcopy(src, dst, ss, rs, dev):
        return pltpu.make_async_remote_copy(
            src_ref=src, dst_ref=dst, send_sem=ss, recv_sem=rs, device_id=dev, device_id_type=MESH
        )

    sends = []

    def go(copy):
        copy.start()
        sends.append(copy)
        return copy

    loads = {}

    def load(name, src, dst):
        copy = pltpu.make_async_copy(src, dst, z.load.at[len(loads)])
        copy.start()
        loads[name] = copy

    load("mem", mem_hbm.at[0], z.held.at[0])
    load("wk", wk_hbm.at[0], z.wk)
    load("stash", stash_hbm.at[0], z.stash)
    load("wq", wq_hbm.at[0], z.wq)
    load("wv", wv_hbm.at[0], z.wv)
    load("grad", grad_hbm.at[0], z.grad)
    load("wo", wo_hbm.at[0], z.wo)

    barrier = pltpu.get_barrier_semaphore()
    senders = [sib, (seg, 2 * c1 + k), (seg, 2 * c3 + k), (nxt3, head)]
    senders += [(nxt, 2 * ((c + r) % 4) + k) for r in range(4)]
    for dev in senders:
        pl.semaphore_signal(barrier, inc=1, device_id=dev, device_id_type=MESH)

    def keys_of(t):
        z.k[t, 0] = joined(wide(z.held[t], z.wk))

    def values_of(t):
        z.v[t, 0] = joined(wide(z.held[t], z.wv))

    def queries_of(t):
        z.q[t] = joined(wide(z.stash[slot_ref[0, t]], z.wq))

    def softmax_of(t, scores, out):
        allowed = lax.broadcasted_iota(jnp.int32, scores[0].shape, 1) < len_ref[0, t]
        weights = []
        for score in scores:
            score = jnp.where(allowed, score, F32(-1e30))
            expo = jnp.exp(score - jnp.max(score, axis=-1, keepdims=True))
            weights.append(expo / jnp.sum(expo, axis=-1, keepdims=True))
        for h, weight in enumerate(weights):
            out[h] = weight

    loads["mem"].wait()
    loads["wk"].wait()
    keys_of(0)
    loads["stash"].wait()
    loads["wq"].wait()
    queries_of(0)

    pl.semaphore_wait(barrier, 8)
    helds = [
        rcopy(z.held.at[t, mine], z.held.at[t + 1, mine], z.h_ss.at[t], z.h_rs.at[t], (prev, head))
        for t in range(TICKS - 1)
    ]
    held_fw = [
        rcopy(z.held.at[t + 1, mine], z.held.at[t + 1, mine], z.hf_ss.at[t], z.hf_rs.at[t], sib)
        for t in range(TICKS - 1)
    ]
    go(helds[0])
    enc_copy = go(rcopy(enc_hbm.at[0], z.encr, z.e_ss, z.e_rs, (prev3, head)))

    softmax_of(0, [nt(z.q[0, :, at(h)], z.k[0, 0, :, at(h)]) for h in range(heads)], z.att)
    loads["wv"].wait()
    values_of(0)
    loads["grad"].wait()
    for j in range(4):
        for u in range(2):
            rows = pl.ds(pl.multiple_of(64 * k + 32 * u, 32), 32)
            z.gres[2 * j + u] = z.grad[rows, 128 * j : 128 * j + 128]
    loads["wo"].wait()

    def keeps(j):
        if j in EARLY:
            side = c
        else:
            side = (c // 2) if (j // 2) % 2 == 0 else ((c + 1) // 2) % 2
        return jnp.where(side == 0, F32(1.0), F32(0.0))

    def partners(j):
        return (c1, c3) if (j // 2) % 2 == 0 else (c3, c1)

    def first_round(t, j, total, first, straight):
        partner = partners(j)[0]
        if j in EARLY:
            total = total + keeps(j) * z.gres[j]
        z.r1s[t, j] = total.astype(BF16)
        section = prev if j in EARLY else seg
        first[j] = go(
            rcopy(
                z.r1s.at[t, j], z.r1r.at[t, j], z.r1_ss.at[t, j], z.r1_rs.at[t, j],
                (section, 2 * partner + k),
            )
        )
        if j in EARLY:
            straight[j] = go(
                rcopy(z.r1s.at[t, j], z.r2x.at[t, j], z.x_ss.at[t, j], z.x_rs.at[t, j], (prev, head))
            )

    def second_round(t, j, first, straight, across):
        partner = partners(j)[1]
        first[j].wait_recv()
        if j in EARLY:
            straight[j].wait_recv()
            total = z.r2x[t, j].astype(F32) + z.r1r[t, j].astype(F32)
        else:
            total = z.r1s[t, j].astype(F32) + z.r1r[t, j].astype(F32) + keeps(j) * z.gres[j]
        z.r2s[t, j] = total.astype(BF16)
        section = seg if j in EARLY else prev
        across[j] = go(
            rcopy(
                z.r2s.at[t, j], z.r2y.at[t, j], z.y_ss.at[t, j], z.y_rs.at[t, j],
                (section, 2 * partner + k),
            )
        )
        if j not in EARLY:
            straight[j] = go(
                rcopy(z.r2s.at[t, j], z.r2x.at[t, j], z.x_ss.at[t, j], z.x_rs.at[t, j], (prev, head))
            )

    def gathered(t, j, straight, across):
        across[j].wait_recv()
        if j in EARLY:
            return z.r2s[t, j].astype(F32) + z.r2y[t, j].astype(F32)
        straight[j].wait_recv()
        return z.r2x[t, j].astype(F32) + z.r2y[t, j].astype(F32)

    weight_copies = []
    shared = None
    for t in range(TICKS):
        last = t == TICKS - 1
        first, straight, across = {}, {}, {}
        if t == 0:
            g = z.grad[...].astype(BF16)
            z.cg[...] = joined(
                [nt(g, z.wo[256 * n : 256 * n + 256, :]).astype(BF16) for n in range(4)]
            )
            prob_grads = [nt(z.cg[:, at(h)], z.v[0, 0, :, at(h)]) for h in range(heads)]
            score_grads = []
            for h in range(heads):
                weight = z.att[h]
                total = jnp.sum(weight * prob_grads[h], axis=-1, keepdims=True)
                score_grads.append((weight * (prob_grads[h] - total)).astype(BF16))
            query_grad = joined(
                [nn(score_grads[h], z.k[0, 0, :, at(h)]).astype(BF16) for h in range(heads)]
            )
            for h in range(heads):
                z.sg[h] = score_grads[h]
            pair = {}
            for n in range(2):
                part = nt(query_grad, z.wq[256 * n : 256 * n + 256, :])
                for j in (2 * n, 2 * n + 1):
                    piece = part[:, 128 * (j - 2 * n) : 128 * (j - 2 * n) + 128]
                    z.dpf[j] = piece
                    z.dpb[j] = piece.astype(BF16)
                    pair[j] = go(
                        rcopy(z.dpb.at[j, other], z.sibr.at[j], z.sib_ss.at[j], z.sib_rs.at[j], sib)
                    )
            for j in FIRST_ORDER:
                pair[j].wait_recv()
                total = z.dpf[j, mine] + z.sibr[j].astype(F32)
                for u in range(2):
                    first_round(t, 2 * j + u, total[32 * u : 32 * u + 32], first, straight)
        else:
            shared[1].wait_recv()
            both = [(h // heads, h % heads) for h in range(2 * heads)]
            prob_grads = [nt(z.cg2[i, :, at(h)], z.v[t, i, :, at(h)]) for i, h in both]
            score_grads = []
            for i, h in both:
                weight = z.att2[heads * i + h]
                total = jnp.sum(weight * prob_grads[heads * i + h], axis=-1, keepdims=True)
                score_grads.append((weight * (prob_grads[heads * i + h] - total)).astype(BF16))
            query_grads = [
                nn(score_grads[heads * i + h], z.k[t, i, :, at(h)]).astype(BF16) for i, h in both
            ]
            for h in range(2 * heads):
                z.sg2[h] = score_grads[h]
            query_grad = [joined(query_grads[:heads]), joined(query_grads[heads:])]
            if t == 1:
                weight_copies[1].wait_recv()
            for n in range(2):
                cols = slice(256 * n, 256 * n + 256)
                part = nn(query_grad[0], z.wqt[0, :, cols]) + nn(query_grad[1], z.wqt[1, :, cols])
                for j in (2 * n, 2 * n + 1):
                    piece = part[:, 128 * (j - 2 * n) : 128 * (j - 2 * n) + 128]
                    for u in range(2):
                        first_round(t, 2 * j + u, piece[32 * u : 32 * u + 32], first, straight)
        if t == 0:
            vgs = [tn(z.att[h].astype(BF16), z.cg[:, at(h)]).astype(BF16) for h in range(heads)]
            kgs = [tn(z.sg[h], z.q[0, :, at(h)]).astype(BF16) for h in range(heads)]
            z.vg[0] = joined(vgs)
            z.kg[0] = joined(kgs)
        else:
            vgs = [
                tn(z.att2[heads * i + h].astype(BF16), z.cg2[i, :, at(h)]).astype(BF16)
                for i, h in both
            ]
            kgs = [
                tn(z.sg2[heads * i + h], z.q[t, mine, at(h)] if i == 0 else z.q2[t, :, at(h)]).astype(
                    BF16
                )
                for i, h in both
            ]
            for i in range(2):
                z.vg[i] = joined(vgs[heads * i : heads * i + heads])
                z.kg[i] = joined(kgs[heads * i : heads * i + heads])
            if t == 1:
                weight_copies[2].wait_recv()
                weight_copies[3].wait_recv()
        for j in range(4):
            rows = slice(128 * j, 128 * j + 128)
            part = nt(z.wk[rows, :], z.kg[0]) + nt(z.wv[rows, :], z.vg[0])
            if t > 0:
                part = part + nt(z.wk2[rows, :], z.kg[1]) + nt(z.wv2[rows, :], z.vg[1])
            z.mpf[j] = part
            z.mpb[t, j] = part.astype(BF16)
        mp_copy = go(rcopy(z.mpb.at[t, :, other], z.mpr.at[t], z.mp_ss.at[t], z.mp_rs.at[t], sib))
        if t == 0:
            for n in range(8):
                z.wot[0, :, at(n)] = z.wo[at(n), :].T
            weight_copies.append(
                go(rcopy(z.wot.at[0], z.wot.at[1], z.w_ss.at[0], z.w_rs.at[0], sib))
            )
            for n in range(8):
                z.wqt[0, at(n), :] = z.wq[:, at(n)].T
            weight_copies.append(
                go(rcopy(z.wqt.at[0], z.wqt.at[1], z.w_ss.at[1], z.w_rs.at[1], sib))
            )
        if not last:
            helds[t].wait_recv()
            go(held_fw[t])
            if t + 1 < TICKS - 1:
                go(helds[t + 1])
            n = t + 1
            queries_of(n)
            queries = rcopy(z.q.at[n, other], z.q2.at[n], z.qq_ss.at[n], z.qq_rs.at[n], sib)
            go(queries)
            held_fw[t].wait_recv()
            keys_of(n)
            shared = [
                go(rcopy(z.k.at[n, 0], z.k.at[n, 1], z.kk_ss.at[n], z.kk_rs.at[n], sib)),
                rcopy(z.v.at[n, 0], z.v.at[n, 1], z.vv_ss.at[n], z.vv_rs.at[n], sib),
            ]
        if t == 0:
            carried = [
                rcopy(z.cs.at[i], z.cr.at[i], z.c_ss.at[i], z.c_rs.at[i], (prev, head))
                for i in range(TICKS - 1)
            ]
        mp_copy.wait_recv()
        if t > 0:
            carried[t - 1].wait_recv()
        for j in range(4):
            part = z.mpf[j, mine] + z.mpr[t, j].astype(F32)
            if t > 0:
                part = part + z.cr[t - 1, j].astype(F32)
            z.cs[t, j] = part.astype(BF16)
        if last:
            final = []
            for r in range(4):
                dest = (c + r) % 4
                final.append(
                    go(
                        rcopy(
                            z.cs.at[t, dest], z.fin.at[r], z.f_ss.at[r], z.f_rs.at[r],
                            (prev, 2 * dest + k),
                        )
                    )
                )
        for j in SECOND_ORDER:
            for u in range(2):
                second_round(t, 2 * j + u, first, straight, across)
        if not last:
            go(carried[t])
        if t == 0:
            for i, (src, dst) in enumerate(((z.wk, z.wk2), (z.wv, z.wv2))):
                weight_copies.append(go(rcopy(src, dst, z.w_ss.at[2 + i], z.w_rs.at[2 + i], sib)))
        if not last:
            values_of(n)
            go(shared[1])
            scores = [nt(z.q[n, mine, at(h)], z.k[n, 0, :, at(h)]) for h in range(heads)]
            queries.wait_recv()
            shared[0].wait_recv()
            scores += [nt(z.q2[n, :, at(h)], z.k[n, 1, :, at(h)]) for h in range(heads)]
            softmax_of(n, scores, z.att2)
            if t == 0:
                weight_copies[0].wait_recv()
            for pair in (SECOND_ORDER[:2], SECOND_ORDER[2:]):
                pieces = []
                for j in pair:
                    totals = []
                    for u in range(2):
                        totals.append(gathered(t, 2 * j + u, straight, across))
                        z.gres[2 * j + u] = totals[u]
                    pieces.append(jnp.concatenate(totals, axis=0).astype(BF16))
                g = joined(pieces)
                for i in range(2):
                    for m in range(z.cgf.shape[2] // 256):
                        cols = slice(256 * m, 256 * m + 256)
                        w = jnp.concatenate([z.wot[i, at(j), cols] for j in pair], axis=0)
                        part = nn(g, w)
                        if pair == SECOND_ORDER[:2]:
                            z.cgf[i, :, cols] = part
                        else:
                            z.cg2[i, :, cols] = (z.cgf[i, :, cols] + part).astype(BF16)
        else:
            forward = {}
            for j in SECOND_ORDER:
                cols = slice(128 * j, 128 * j + 128)
                gout_ref[0, mine, cols] = jnp.concatenate(
                    [gathered(t, 2 * j + u, straight, across) for u in range(2)], axis=0
                )
                forward[j] = go(
                    rcopy(
                        gout_ref.at[0, mine, cols], z.gfin.at[j], z.fw_ss.at[j], z.fw_rs.at[j], sib
                    )
                )
            for r in range(4):
                final[r].wait_recv()
            enc_copy.wait_recv()
            eout_ref[0] = (
                z.encr[...]
                + (z.fin[0].astype(F32) + z.fin[1].astype(F32))
                + (z.fin[2].astype(F32) + z.fin[3].astype(F32))
            )
            for j in SECOND_ORDER:
                forward[j].wait_recv()
                gout_ref[0, other, 128 * j : 128 * j + 128] = z.gfin[j]

    for copy in sends:
        copy.wait_send()


def body(
    grad_in, memory, enc_grad_in, act_stash, slot_order, lengths, w_query, w_key, w_value, w_out
):
    anywhere = pl.BlockSpec(memory_space=pl.ANY)
    scalars = pl.BlockSpec(memory_space=pltpu.SMEM)
    whole = pl.BlockSpec(memory_space=pltpu.VMEM)
    spec = scratch_spec(w_query.shape[2])
    names = tuple(spec)
    enc_turned = jnp.swapaxes(enc_grad_in, 1, 2)

    def relay(*refs):
        kernel(names, *refs)

    grad_out, enc_out = pl.pallas_call(
        relay,
        name="relay_backward",
        out_shape=(
            jax.ShapeDtypeStruct(grad_in.shape, F32),
            jax.ShapeDtypeStruct(enc_turned.shape, F32),
        ),
        in_specs=[anywhere] * 4 + [scalars] * 2 + [anywhere] * 4,
        out_specs=(whole, whole),
        scratch_shapes=list(spec.values()),
        compiler_params=pltpu.CompilerParams(
            collective_id=0, has_side_effects=True, vmem_limit_bytes=56 * 1024 * 1024
        ),
        cost_estimate=pl.CostEstimate(
            flops=3_400_000_000, bytes_accessed=5_500_000, transcendentals=400_000
        ),
    )(grad_in, memory, enc_turned, act_stash, slot_order, lengths, w_query, w_key, w_value, w_out)
    return grad_out, jnp.swapaxes(enc_out, 1, 2)


def solution(mesh):
    in_specs = (
        P("segment", None, None),
        P("segment", None, None),
        P("segment", None, "head"),
        P("segment", None, None, None),
        P("segment", None),
        P("segment", None),
        P("segment", None, "head"),
        P("segment", None, "head"),
        P("segment", None, "head"),
        P("segment", "head", None),
    )
    out_specs = (P("segment", None, None), P("segment", None, "head"))
    return jax.shard_map(body, mesh=mesh, in_specs=in_specs, out_specs=out_specs, check_vma=False)
```

```python
import types

import jax
import jax.numpy as jnp
from jax import lax
from jax.experimental import pallas as pl
from jax.experimental.pallas import tpu as pltpu
from jax.sharding import PartitionSpec as P

HEAD_DIM = 128
TICKS = 3
MESH = pl.DeviceIdType.MESH
F32 = jnp.float32
BF16 = jnp.bfloat16
EARLY = ()
FIRST_ORDER = (0, 1, 2, 3)
SECOND_ORDER = (0, 1, 2, 3)


def nn(a, b):
    return lax.dot_general(a, b, (((1,), (0,)), ((), ())), preferred_element_type=F32)


def nt(a, b):
    return lax.dot_general(a, b, (((1,), (1,)), ((), ())), preferred_element_type=F32)


def tn(a, b):
    return lax.dot_general(a, b, (((0,), (0,)), ((), ())), preferred_element_type=F32)


def at(h):
    return slice(HEAD_DIM * h, HEAD_DIM * h + HEAD_DIM)


def wide(a, w):
    return [nn(a, w[:, 256 * n : 256 * n + 256]).astype(BF16) for n in range(w.shape[1] // 256)]


def joined(pieces):
    return jnp.concatenate(pieces, axis=1)


def scratch_spec(inner):
    heads = inner // HEAD_DIM
    half = (64, 128)

    def v(shape, kind):
        return pltpu.VMEM(shape, kind)

    def s(*shape):
        return pltpu.SemaphoreType.DMA(shape) if shape else pltpu.SemaphoreType.DMA

    spec = dict(
        grad=v((128, 512), F32), stash=v((TICKS, 128, 512), BF16),
        wq=v((512, inner), BF16), wk=v((512, inner), BF16), wv=v((512, inner), BF16),
        wo=v((inner, 512), BF16), wot=v((2, 512, inner), BF16), wqt=v((2, inner, 512), BF16),
        wk2=v((512, inner), BF16), wv2=v((512, inner), BF16),
        held=v((TICKS, 128, 512), BF16),
        q=v((TICKS, 128, inner), BF16), k=v((TICKS, 2, 128, inner), BF16),
        v=v((TICKS, 2, 128, inner), BF16), q2=v((TICKS, 64, inner), BF16),
        att=v((heads, 128, 128), F32), att2=v((2 * heads, 64, 128), F32),
        cg=v((128, inner), BF16), sg=v((heads, 128, 128), BF16),
        cg2=v((2, 64, inner), BF16), cgf=v((2, 64, inner), F32), sg2=v((2 * heads, 64, 128), BF16),
        kg=v((2, 128, inner), BF16), vg=v((2, 128, inner), BF16),
        gres=v((8, 32, 128), F32), dpf=v((4, 128, 128), F32), dpb=v((4, 128, 128), BF16),
        sibr=v((4, *half), BF16),
        r1s=v((TICKS, 8, 32, 128), BF16), r1r=v((TICKS, 8, 32, 128), BF16),
        r2s=v((TICKS, 8, 32, 128), BF16), r2x=v((TICKS, 8, 32, 128), BF16),
        r2y=v((TICKS, 8, 32, 128), BF16), gfin=v((4, *half), F32),
        mpf=v((4, 128, 128), F32), mpb=v((TICKS, 4, 128, 128), BF16),
        mpr=v((TICKS, 4, *half), BF16), cs=v((TICKS, 4, *half), BF16),
        cr=v((TICKS - 1, 4, *half), BF16), fin=v((4, *half), BF16), encr=v(half, F32),
        load=s(7),
    )
    for name, shape in dict(
        sib=(4,), r1=(TICKS, 8), x=(TICKS, 8), y=(TICKS, 8), fw=(4,), mp=(TICKS,), c=(TICKS - 1,),
        f=(4,), h=(TICKS - 1,), hf=(TICKS - 1,), e=(), w=(4,), kk=(TICKS,), vv=(TICKS,), qq=(TICKS,),
    ).items():
        spec[name + "_ss"] = s(*shape)
        spec[name + "_rs"] = s(*shape)
    return spec


def kernel(
    names, grad_hbm, mem_hbm, enc_hbm, stash_hbm, slot_ref, len_ref, wq_hbm, wk_hbm, wv_hbm, wo_hbm,
    gout_ref, eout_ref, *scratch
):
    z = types.SimpleNamespace(**dict(zip(names, scratch)))
    heads = z.wq.shape[1] // HEAD_DIM
    seg = lax.axis_index("segment")
    head = lax.axis_index("head")
    segments = lax.axis_size("segment")
    c = head // 2
    k = head % 2
    prev = (seg + segments - 1) % segments
    prev3 = (seg + 3 * segments - 3) % segments
    nxt = (seg + 1) % segments
    nxt3 = (seg + 3) % segments
    c1 = c + 1 - 2 * (c % 2)
    c3 = 3 - c
    sib = (seg, 2 * c + 1 - k)
    mine = pl.ds(pl.multiple_of(64 * k, 64), 64)
    other = pl.ds(pl.multiple_of(64 * (1 - k), 64), 64)

    def rcopy(src, dst, ss, rs, dev):
        return pltpu.make_async_remote_copy(
            src_ref=src, dst_ref=dst, send_sem=ss, recv_sem=rs, device_id=dev, device_id_type=MESH
        )

    sends = []

    def go(copy):
        copy.start()
        sends.append(copy)
        return copy

    loads = {}

    def load(name, src, dst):
        copy = pltpu.make_async_copy(src, dst, z.load.at[len(loads)])
        copy.start()
        loads[name] = copy

    load("mem", mem_hbm.at[0], z.held.at[0])
    load("wk", wk_hbm.at[0], z.wk)
    load("stash", stash_hbm.at[0], z.stash)
    load("wq", wq_hbm.at[0], z.wq)
    load("wv", wv_hbm.at[0], z.wv)
    load("grad", grad_hbm.at[0], z.grad)
    load("wo", wo_hbm.at[0], z.wo)

    barrier = pltpu.get_barrier_semaphore()
    senders = [sib, (seg, 2 * c1 + k), (seg, 2 * c3 + k), (nxt3, head)]
    senders += [(nxt, 2 * ((c + r) % 4) + k) for r in range(4)]
    for dev in senders:
        pl.semaphore_signal(barrier, inc=1, device_id=dev, device_id_type=MESH)

    def keys_of(t):
        z.k[t, 0] = joined(wide(z.held[t], z.wk))

    def values_of(t):
        z.v[t, 0] = joined(wide(z.held[t], z.wv))

    def queries_of(t):
        z.q[t] = joined(wide(z.stash[slot_ref[0, t]], z.wq))

    def softmax_of(t, scores, out):
        allowed = lax.broadcasted_iota(jnp.int32, scores[0].shape, 1) < len_ref[0, t]
        weights = []
        for score in scores:
            score = jnp.where(allowed, score, F32(-1e30))
            expo = jnp.exp(score - jnp.max(score, axis=-1, keepdims=True))
            weights.append(expo / jnp.sum(expo, axis=-1, keepdims=True))
        for h, weight in enumerate(weights):
            out[h] = weight

    loads["mem"].wait()
    loads["wk"].wait()
    keys_of(0)
    loads["stash"].wait()
    loads["wq"].wait()
    queries_of(0)

    helds = [
        rcopy(z.held.at[t, mine], z.held.at[t + 1, mine], z.h_ss.at[t], z.h_rs.at[t], (prev, head))
        for t in range(TICKS - 1)
    ]
    held_fw = [
        rcopy(z.held.at[t + 1, mine], z.held.at[t + 1, mine], z.hf_ss.at[t], z.hf_rs.at[t], sib)
        for t in range(TICKS - 1)
    ]
    enc_copy = rcopy(enc_hbm.at[0], z.encr, z.e_ss, z.e_rs, (prev3, head))

    softmax_of(0, [nt(z.q[0, :, at(h)], z.k[0, 0, :, at(h)]) for h in range(heads)], z.att)
    loads["wv"].wait()
    values_of(0)
    loads["grad"].wait()
    for j in range(4):
        for u in range(2):
            rows = pl.ds(pl.multiple_of(64 * k + 32 * u, 32), 32)
            z.gres[2 * j + u] = z.grad[rows, 128 * j : 128 * j + 128]
    loads["wo"].wait()

    def keeps(j):
        if j in EARLY:
            side = c
        else:
            side = (c // 2) if (j // 2) % 2 == 0 else ((c + 1) // 2) % 2
        return jnp.where(side == 0, F32(1.0), F32(0.0))

    def partners(j):
        return (c1, c3) if (j // 2) % 2 == 0 else (c3, c1)

    def first_round(t, j, total, first, straight):
        partner = partners(j)[0]
        if j in EARLY:
            total = total + keeps(j) * z.gres[j]
        z.r1s[t, j] = total.astype(BF16)
        section = prev if j in EARLY else seg
        first[j] = go(
            rcopy(
                z.r1s.at[t, j], z.r1r.at[t, j], z.r1_ss.at[t, j], z.r1_rs.at[t, j],
                (section, 2 * partner + k),
            )
        )
        if j in EARLY:
            straight[j] = go(
                rcopy(z.r1s.at[t, j], z.r2x.at[t, j], z.x_ss.at[t, j], z.x_rs.at[t, j], (prev, head))
            )

    def second_round(t, j, first, straight, across):
        partner = partners(j)[1]
        first[j].wait_recv()
        if j in EARLY:
            straight[j].wait_recv()
            total = z.r2x[t, j].astype(F32) + z.r1r[t, j].astype(F32)
        else:
            total = z.r1s[t, j].astype(F32) + z.r1r[t, j].astype(F32) + keeps(j) * z.gres[j]
        z.r2s[t, j] = total.astype(BF16)
        section = seg if j in EARLY else prev
        across[j] = go(
            rcopy(
                z.r2s.at[t, j], z.r2y.at[t, j], z.y_ss.at[t, j], z.y_rs.at[t, j],
                (section, 2 * partner + k),
            )
        )
        if j not in EARLY:
            straight[j] = go(
                rcopy(z.r2s.at[t, j], z.r2x.at[t, j], z.x_ss.at[t, j], z.x_rs.at[t, j], (prev, head))
            )

    def gathered(t, j, straight, across):
        across[j].wait_recv()
        if j in EARLY:
            return z.r2s[t, j].astype(F32) + z.r2y[t, j].astype(F32)
        straight[j].wait_recv()
        return z.r2x[t, j].astype(F32) + z.r2y[t, j].astype(F32)

    weight_copies = []
    shared = None
    for t in range(TICKS):
        last = t == TICKS - 1
        first, straight, across = {}, {}, {}
        if t == 0:
            g = z.grad[...].astype(BF16)
            z.cg[...] = joined(
                [nt(g, z.wo[256 * n : 256 * n + 256, :]).astype(BF16) for n in range(4)]
            )
            prob_grads = [nt(z.cg[:, at(h)], z.v[0, 0, :, at(h)]) for h in range(heads)]
            score_grads = []
            for h in range(heads):
                weight = z.att[h]
                total = jnp.sum(weight * prob_grads[h], axis=-1, keepdims=True)
                score_grads.append((weight * (prob_grads[h] - total)).astype(BF16))
            query_grad = joined(
                [nn(score_grads[h], z.k[0, 0, :, at(h)]).astype(BF16) for h in range(heads)]
            )
            for h in range(heads):
                z.sg[h] = score_grads[h]
            for n in range(2):
                part = nt(query_grad, z.wq[256 * n : 256 * n + 256, :])
                for j in (2 * n, 2 * n + 1):
                    piece = part[:, 128 * (j - 2 * n) : 128 * (j - 2 * n) + 128]
                    z.dpf[j] = piece
                    z.dpb[j] = piece.astype(BF16)
            pl.semaphore_wait(barrier, 8)
            pair = {}
            for j in FIRST_ORDER:
                pair[j] = go(
                    rcopy(z.dpb.at[j, other], z.sibr.at[j], z.sib_ss.at[j], z.sib_rs.at[j], sib)
                )
            go(helds[0])
            go(enc_copy)
            for j in FIRST_ORDER:
                pair[j].wait_recv()
                total = z.dpf[j, mine] + z.sibr[j].astype(F32)
                for u in range(2):
                    first_round(t, 2 * j + u, total[32 * u : 32 * u + 32], first, straight)
        else:
            shared[1].wait_recv()
            both = [(h // heads, h % heads) for h in range(2 * heads)]
            prob_grads = [nt(z.cg2[i, :, at(h)], z.v[t, i, :, at(h)]) for i, h in both]
            score_grads = []
            for i, h in both:
                weight = z.att2[heads * i + h]
                total = jnp.sum(weight * prob_grads[heads * i + h], axis=-1, keepdims=True)
                score_grads.append((weight * (prob_grads[heads * i + h] - total)).astype(BF16))
            query_grads = [
                nn(score_grads[heads * i + h], z.k[t, i, :, at(h)]).astype(BF16) for i, h in both
            ]
            for h in range(2 * heads):
                z.sg2[h] = score_grads[h]
            query_grad = [joined(query_grads[:heads]), joined(query_grads[heads:])]
            if t == 1:
                weight_copies[1].wait_recv()
            for n in range(2):
                cols = slice(256 * n, 256 * n + 256)
                part = nn(query_grad[0], z.wqt[0, :, cols]) + nn(query_grad[1], z.wqt[1, :, cols])
                for j in (2 * n, 2 * n + 1):
                    piece = part[:, 128 * (j - 2 * n) : 128 * (j - 2 * n) + 128]
                    for u in range(2):
                        first_round(t, 2 * j + u, piece[32 * u : 32 * u + 32], first, straight)
        if t == 0:
            vgs = [tn(z.att[h].astype(BF16), z.cg[:, at(h)]).astype(BF16) for h in range(heads)]
            kgs = [tn(z.sg[h], z.q[0, :, at(h)]).astype(BF16) for h in range(heads)]
            z.vg[0] = joined(vgs)
            z.kg[0] = joined(kgs)
        else:
            vgs = [
                tn(z.att2[heads * i + h].astype(BF16), z.cg2[i, :, at(h)]).astype(BF16)
                for i, h in both
            ]
            kgs = [
                tn(z.sg2[heads * i + h], z.q[t, mine, at(h)] if i == 0 else z.q2[t, :, at(h)]).astype(
                    BF16
                )
                for i, h in both
            ]
            for i in range(2):
                z.vg[i] = joined(vgs[heads * i : heads * i + heads])
                z.kg[i] = joined(kgs[heads * i : heads * i + heads])
            if t == 1:
                weight_copies[2].wait_recv()
                weight_copies[3].wait_recv()
        for j in range(4):
            rows = slice(128 * j, 128 * j + 128)
            part = nt(z.wk[rows, :], z.kg[0]) + nt(z.wv[rows, :], z.vg[0])
            if t > 0:
                part = part + nt(z.wk2[rows, :], z.kg[1]) + nt(z.wv2[rows, :], z.vg[1])
            z.mpf[j] = part
            z.mpb[t, j] = part.astype(BF16)
        mp_copy = go(rcopy(z.mpb.at[t, :, other], z.mpr.at[t], z.mp_ss.at[t], z.mp_rs.at[t], sib))
        if t == 0:
            for n in range(8):
                z.wot[0, :, at(n)] = z.wo[at(n), :].T
            weight_copies.append(
                go(rcopy(z.wot.at[0], z.wot.at[1], z.w_ss.at[0], z.w_rs.at[0], sib))
            )
            for n in range(8):
                z.wqt[0, at(n), :] = z.wq[:, at(n)].T
            weight_copies.append(
                go(rcopy(z.wqt.at[0], z.wqt.at[1], z.w_ss.at[1], z.w_rs.at[1], sib))
            )
        if not last:
            n = t + 1
            queries_of(n)
            queries = rcopy(z.q.at[n, other], z.q2.at[n], z.qq_ss.at[n], z.qq_rs.at[n], sib)
            if t > 0:
                helds[t].wait_recv()
                go(held_fw[t])
            go(queries)
            if t > 0:
                held_fw[t].wait_recv()
                keys_of(n)
                shared = [
                    go(rcopy(z.k.at[n, 0], z.k.at[n, 1], z.kk_ss.at[n], z.kk_rs.at[n], sib)),
                    rcopy(z.v.at[n, 0], z.v.at[n, 1], z.vv_ss.at[n], z.vv_rs.at[n], sib),
                ]
        if t == 0:
            carried = [
                rcopy(z.cs.at[i], z.cr.at[i], z.c_ss.at[i], z.c_rs.at[i], (prev, head))
                for i in range(TICKS - 1)
            ]
        mp_copy.wait_recv()
        if t > 0:
            carried[t - 1].wait_recv()
        for j in range(4):
            part = z.mpf[j, mine] + z.mpr[t, j].astype(F32)
            if t > 0:
                part = part + z.cr[t - 1, j].astype(F32)
            z.cs[t, j] = part.astype(BF16)
        if last:
            final = []
            for r in range(4):
                dest = (c + r) % 4
                final.append(
                    go(
                        rcopy(
                            z.cs.at[t, dest], z.fin.at[r], z.f_ss.at[r], z.f_rs.at[r],
                            (prev, 2 * dest + k),
                        )
                    )
                )
        if t == 0:
            helds[t].wait_recv()
            go(held_fw[t])
        for j in SECOND_ORDER:
            for u in range(2):
                second_round(t, 2 * j + u, first, straight, across)
        if not last:
            go(carried[t])
        if t == 0:
            for i, (src, dst) in enumerate(((z.wk, z.wk2), (z.wv, z.wv2))):
                weight_copies.append(go(rcopy(src, dst, z.w_ss.at[2 + i], z.w_rs.at[2 + i], sib)))
        if not last:
            if n < TICKS - 1:
                go(helds[n])
            if t == 0:
                held_fw[t].wait_recv()
                keys_of(n)
                shared = [
                    go(rcopy(z.k.at[n, 0], z.k.at[n, 1], z.kk_ss.at[n], z.kk_rs.at[n], sib)),
                    rcopy(z.v.at[n, 0], z.v.at[n, 1], z.vv_ss.at[n], z.vv_rs.at[n], sib),
                ]
            values_of(n)
            go(shared[1])
            scores = [nt(z.q[n, mine, at(h)], z.k[n, 0, :, at(h)]) for h in range(heads)]
            queries.wait_recv()
            shared[0].wait_recv()
            scores += [nt(z.q2[n, :, at(h)], z.k[n, 1, :, at(h)]) for h in range(heads)]
            softmax_of(n, scores, z.att2)
            if t == 0:
                weight_copies[0].wait_recv()
            for pair in (SECOND_ORDER[:2], SECOND_ORDER[2:]):
                pieces = []
                for j in pair:
                    totals = []
                    for u in range(2):
                        totals.append(gathered(t, 2 * j + u, straight, across))
                        z.gres[2 * j + u] = totals[u]
                    pieces.append(jnp.concatenate(totals, axis=0).astype(BF16))
                g = joined(pieces)
                for i in range(2):
                    for m in range(z.cgf.shape[2] // 256):
                        cols = slice(256 * m, 256 * m + 256)
                        w = jnp.concatenate([z.wot[i, at(j), cols] for j in pair], axis=0)
                        part = nn(g, w)
                        if pair == SECOND_ORDER[:2]:
                            z.cgf[i, :, cols] = part
                        else:
                            z.cg2[i, :, cols] = (z.cgf[i, :, cols] + part).astype(BF16)
        else:
            forward = {}
            for j in SECOND_ORDER:
                cols = slice(128 * j, 128 * j + 128)
                gout_ref[0, mine, cols] = jnp.concatenate(
                    [gathered(t, 2 * j + u, straight, across) for u in range(2)], axis=0
                )
                forward[j] = go(
                    rcopy(
                        gout_ref.at[0, mine, cols], z.gfin.at[j], z.fw_ss.at[j], z.fw_rs.at[j], sib
                    )
                )
            for r in range(4):
                final[r].wait_recv()
            enc_copy.wait_recv()
            eout_ref[0] = (
                z.encr[...]
                + (z.fin[0].astype(F32) + z.fin[1].astype(F32))
                + (z.fin[2].astype(F32) + z.fin[3].astype(F32))
            )
            for j in SECOND_ORDER:
                forward[j].wait_recv()
                gout_ref[0, other, 128 * j : 128 * j + 128] = z.gfin[j]

    for copy in sends:
        copy.wait_send()


def body(
    grad_in, memory, enc_grad_in, act_stash, slot_order, lengths, w_query, w_key, w_value, w_out
):
    anywhere = pl.BlockSpec(memory_space=pl.ANY)
    scalars = pl.BlockSpec(memory_space=pltpu.SMEM)
    whole = pl.BlockSpec(memory_space=pltpu.VMEM)
    spec = scratch_spec(w_query.shape[2])
    names = tuple(spec)
    enc_turned = jnp.swapaxes(enc_grad_in, 1, 2)

    def relay(*refs):
        kernel(names, *refs)

    grad_out, enc_out = pl.pallas_call(
        relay,
        name="relay_backward",
        out_shape=(
            jax.ShapeDtypeStruct(grad_in.shape, F32),
            jax.ShapeDtypeStruct(enc_turned.shape, F32),
        ),
        in_specs=[anywhere] * 4 + [scalars] * 2 + [anywhere] * 4,
        out_specs=(whole, whole),
        scratch_shapes=list(spec.values()),
        compiler_params=pltpu.CompilerParams(
            collective_id=0, has_side_effects=True, vmem_limit_bytes=56 * 1024 * 1024
        ),
        cost_estimate=pl.CostEstimate(
            flops=3_400_000_000, bytes_accessed=5_500_000, transcendentals=400_000
        ),
    )(grad_in, memory, enc_turned, act_stash, slot_order, lengths, w_query, w_key, w_value, w_out)
    return grad_out, jnp.swapaxes(enc_out, 1, 2)


def solution(mesh):
    in_specs = (
        P("segment", None, None),
        P("segment", None, None),
        P("segment", None, "head"),
        P("segment", None, None, None),
        P("segment", None),
        P("segment", None),
        P("segment", None, "head"),
        P("segment", None, "head"),
        P("segment", None, "head"),
        P("segment", "head", None),
    )
    out_specs = (P("segment", None, None), P("segment", None, "head"))
    return jax.shard_map(body, mesh=mesh, in_specs=in_specs, out_specs=out_specs, check_vma=False)
```
